256 devices in a mesh: band: 16 (over z, y_lo), gblk: 16 (over x, y_hi, core).
Axes of the slice: x: 4, y: 4 (y_hi: 2, y_lo: 2; y = y_hi * 2 + y_lo), z: 8, core: 2. Of those that a mesh axis runs over, the one named last changes fastest.
Arguments:
- psi_val: bfloat16 [128, 1024], P('band'), may hold values from -6 to 6
- psi_con: bfloat16 [64, 1024], P('band'), may hold values from -6 to 6
- val_energy: float32 [128], P('band'), may hold values from -12 to -1
- con_energy: float32 [64], P('band'), may hold values from 1 to 30
- sphere_basis: bfloat16 [1024, 61440], P(None, 'gblk'), may hold values from -0.1875 to 0.1875
- block_owner: int32 [480], replicated, may hold values from 0 to 15, as said below
- block_fill: int32 [480], replicated, may hold values from 32 to 128
Outputs:
- polarizability: float32 [98304, 256], P('gblk', 'band')
The draws below stay inside these ranges and needn't reach their ends.
Inputs may be any that keep to these rules, and one draw needn't show every extreme that they name: `block_owner`: producer p holds blocks p * 480 / 16 onward; it gives at most 3 of them to any owner, and one owner receives exactly 3 from every producer.
All inputs are finite; a program needn't handle non-finite values.
Results may differ from the reference program's by a relative error of at most 0.008.
Values may be sent and summed in bfloat16 or wider, within the bound.
A program may use at most 128 MiB of HBM per device.

```python
import math
import jax
import jax.numpy as jnp
from jax import lax

NV = 128
R = 1024
W = 256
BLK = 128
NBLK = 480
NC = 64
CAP = 3
N_GBLK = 16


def draw_block_owner(key, part):
    key = jax.random.fold_in(key, 11)
    pick_key, bias_key, noise_key, shuffle_key = jax.random.split(key, 4)
    per_prod = NBLK // N_GBLK
    listed = N_GBLK * CAP
    owners = jnp.arange(listed, dtype=jnp.int32) // CAP
    favoured = jax.random.randint(pick_key, (), 0, N_GBLK)
    weights = jax.random.randint(bias_key, (N_GBLK,), 0, 4)
    noise = jax.random.randint(noise_key, (N_GBLK, listed), 0, 4096)
    score = noise - 1024 * weights[owners][None, :]
    score = jnp.where(owners[None, :] == favoured, -8192, score)
    score = score * listed + jnp.arange(listed, dtype=jnp.int32)[None, :]
    order = jnp.argsort(score, axis=1)
    chosen = owners[order[:, :per_prod]]
    mixing = jax.random.randint(shuffle_key, (N_GBLK, per_prod), 0, 4096)
    mixing = mixing * per_prod + jnp.arange(per_prod, dtype=jnp.int32)[None, :]
    shuffle = jnp.argsort(mixing, axis=1)
    chosen = jnp.take_along_axis(chosen, shuffle, axis=1)
    return chosen.reshape(NBLK).astype(jnp.int32)


def draw_block_fill(key, part):
    key = jax.random.fold_in(key, 23)
    fill_key, top_key, low_key = jax.random.split(key, 3)
    filled = jnp.minimum(jax.random.randint(fill_key, (NBLK,), BLK // 4, BLK + BLK // 2), BLK)
    top_block = jax.random.randint(top_key, (), 0, NBLK)
    low_block = (top_block + 1 + jax.random.randint(low_key, (), 0, NBLK - 1)) % NBLK
    filled = filled.at[top_block].set(BLK).at[low_block].set(BLK // 4)
    return filled.astype(jnp.int32)


def block_levels(rng, extent, cuts, low, largest):
    gain, own = 1.0, jax.random.fold_in(rng, 6)
    for position, parts in cuts:
        steps = jnp.exp(jax.random.uniform(jax.random.fold_in(own, position), (parts,), jnp.float32, low / len(cuts), largest / len(cuts)))
        gain = gain * jnp.repeat(steps, extent[position] // parts).reshape([-1 if axis == position else 1 for axis in range(len(extent))])
    return gain


def normal_values(rng, dims, scale, reach, shards=(), held_as=jnp.bfloat16):
    entries = jax.random.normal(rng, dims, jnp.float32) * scale
    if len(shards) > 0:
        entries = block_levels(rng, dims, shards, -0.22, 0.18) * entries
    return jnp.clip(entries, min=-reach, max=reach).astype(held_as)


def setup_inputs(seed: int = 0) -> dict:
    splits = jax.random.split(jax.random.key(seed), 8)
    return {
        "psi_val": normal_values(splits[0], (NV, R), 1.0, 6.0, ((0, 16),)),
        "psi_con": normal_values(splits[1], (NC, R), 1.0, 6.0, ((0, 16),)),
        "val_energy": jnp.clip(-12.0 + 11.0 * jax.random.uniform(splits[2], (NV,), jnp.float32) ** block_levels(splits[2], (NV,), ((0, 16),), -0.2, 0.2), -12.0, -1.0),
        "con_energy": jnp.clip(1.0 + 29.0 * jax.random.uniform(splits[3], (NC,), jnp.float32) ** block_levels(splits[3], (NC,), ((0, 16),), -0.2, 0.2), 1.0, 30.0),
        "sphere_basis": normal_values(splits[4], (R, NBLK * BLK), R ** -0.5, 0.1875, ((1, 16),)),
        "block_owner": draw_block_owner(jax.random.fold_in(splits[7], 71), 0),
        "block_fill": draw_block_fill(jax.random.fold_in(splits[7], 71), 0),
    }


def block_ranks(owner_table):
    block_cols = owner_table.shape[1]
    same_owner = owner_table[:, :, None] == owner_table[:, None, :]
    earlier = jnp.arange(block_cols)[None, :] < jnp.arange(block_cols)[:, None]
    return lax.optimization_barrier(jnp.sum((same_owner & earlier[None]).astype(jnp.int32), axis=2))

def reference(psi_val, psi_con, val_energy, con_energy, sphere_basis, block_owner, block_fill):
    val_total = psi_val.shape[0]
    con_total = psi_con.shape[0]
    factor = 1.0 / math.sqrt(val_total * con_total)
    live_mask = (jnp.arange(BLK)[None, :] < block_fill[:, None]).astype(jnp.float32).reshape(-1)
    conduction = psi_con.astype(jnp.float32)

    def one_band(running, inputs):
        orbital, energy = inputs
        pair_rows = (orbital.astype(jnp.float32)[None, :] * conduction).astype(jnp.bfloat16)
        densities = (jnp.dot(pair_rows, sphere_basis, preferred_element_type=jnp.float32) * live_mask).astype(jnp.bfloat16)
        weight = factor / (energy - con_energy)
        scaled = (weight[:, None] * densities[:, :W].astype(jnp.float32)).astype(jnp.bfloat16)
        update = lax.dot_general(densities, scaled, (((0,), (0,)), ((), ())), preferred_element_type=jnp.float32)
        return (running + update, None)
    start = jnp.zeros((NBLK * BLK, W), jnp.float32)
    chi_full, _ = lax.scan(one_band, start, (psi_val, val_energy))
    blocks_local = NBLK // N_GBLK
    owner_table = block_owner.reshape(N_GBLK, blocks_local)
    rank_table = block_ranks(owner_table)
    owner_ids = jnp.arange(N_GBLK).astype(jnp.int32)
    slot_ids = jnp.arange(CAP).astype(jnp.int32)
    matched = (owner_table[None, :, None, :] == owner_ids[:, None, None, None]) & (rank_table[None, :, None, :] == slot_ids[None, None, :, None])
    block_index = lax.optimization_barrier(jnp.sum(matched.astype(jnp.int32) * jnp.arange(blocks_local).astype(jnp.int32), axis=3))
    block_index = block_index + (jnp.arange(N_GBLK).astype(jnp.int32) * blocks_local)[None, :, None]
    present = jnp.any(matched, axis=3).astype(jnp.float32)
    blocks = chi_full.reshape(NBLK, BLK, W)
    picked = blocks[block_index] * present[:, :, :, None, None]
    return picked.reshape(N_GBLK * N_GBLK * CAP * BLK, W)
```

```python
import functools
import math

import jax
import jax.numpy as jnp
from jax import lax
from jax.experimental import pallas as pl
from jax.experimental.pallas import tpu as pltpu
from jax.sharding import PartitionSpec as P

BLK = 128
CAP = 3
GROUP = 16
VAL = 8
CON = 4

f32 = jnp.float32
bf16 = jnp.bfloat16


def band_order(n):
    def hops(d):
        z = (d // 2) % 8
        return min(z, 8 - z) + d % 2

    return sorted(range(1, n), key=lambda d: -hops(d))


def gblk_order(n):
    def hops(d):
        x = d // 4
        return min(x, 4 - x) + 2 * ((d // 2) % 2) + d % 2

    return sorted(range(1, n), key=lambda d: -hops(d))


def kernel(
    nb,
    ng,
    factor,
    val_hbm,
    con_hbm,
    ve_ref,
    ce_ref,
    owner_ref,
    fill_ref,
    table_hbm,
    out_ref,
    val_v,
    con_v,
    table_v,
    win_v,
    psi,
    turned,
    bw,
    con_f,
    x_s,
    s_s,
    m_s,
    chi,
    send,
    slot_s,
    ld_sem,
    gs_sem,
    gr_sem,
    fs_sem,
    fr_sem,
    ws_sem,
    wr_sem,
    cs_sem,
    cr_sem,
    own_sem,
):
    b = lax.axis_index("band")
    p = lax.axis_index("gblk")
    core = lax.rem(p, 2)
    partner = p + 1 - 2 * core
    r = psi.shape[1]
    half = r // 2
    cols = table_v.shape[1]
    blocks = cols // BLK
    border = band_order(nb)
    gorder = gblk_order(ng)

    barrier = pltpu.get_barrier_semaphore()
    for d in border:
        pl.semaphore_signal(barrier, 1, device_id={"band": lax.rem(b + d, nb)})
    for d in gorder:
        pl.semaphore_signal(barrier, 1, device_id={"gblk": lax.rem(p + d, ng)})

    ld_val = pltpu.make_async_copy(val_hbm, val_v, ld_sem.at[0])
    ld_con = pltpu.make_async_copy(con_hbm, con_v, ld_sem.at[1])
    ld_val.start()
    ld_con.start()
    wcol = pl.multiple_of((b // 8) * BLK, BLK)

    def win_copy():
        return pltpu.make_async_copy(
            table_hbm.at[:, pl.ds(wcol, BLK)], win_v, ld_sem.at[3]
        )

    @pl.when(p == 0)
    def _():
        win_copy().start()

    ld_table = pltpu.make_async_copy(table_hbm, table_v, ld_sem.at[2])
    ld_table.start()

    lane = lax.broadcasted_iota(jnp.int32, (1, 256), 1)
    energy = jnp.zeros((1, 256), f32)
    for j in range(VAL):
        energy = jnp.where(lane % GROUP == j, ve_ref[j], energy)
    for j in range(CON):
        energy = jnp.where(lane % GROUP == VAL + j, ce_ref[j], energy)
    hi = energy.astype(bf16).astype(f32)
    mid = (energy - hi).astype(bf16).astype(f32)
    lo = energy - hi - mid
    parts = jnp.concatenate([hi, mid, lo, jnp.zeros_like(hi)], axis=0)
    parts = jnp.concatenate([parts, jnp.zeros((4, r - 256), f32)], axis=1)
    ld_val.wait()
    ld_con.wait()
    mine = jnp.concatenate([val_v[...].astype(f32), con_v[...].astype(f32), parts], axis=0)
    my_rows = pl.ds(pl.multiple_of(b * GROUP, GROUP), GROUP)
    psi[my_rows, :] = mine.astype(bf16)

    @pl.when(p == 0)
    def _():
        win_copy().wait()
        turned[...] = win_v[...].astype(f32).T
        bw[...] = turned[pl.ds(pl.multiple_of(lax.rem(b, 8) * 16, 16), 16), :].astype(bf16)

    pl.semaphore_wait(barrier, nb + ng - 2)

    my_cols = pl.ds(pl.multiple_of(core * half, half), half)

    def gather_copy(i, group):
        rows = pl.ds(pl.multiple_of(group * GROUP, GROUP), GROUP)
        return pltpu.make_async_remote_copy(
            src_ref=psi.at[rows, my_cols],
            dst_ref=psi.at[rows, my_cols],
            send_sem=gs_sem.at[i],
            recv_sem=gr_sem.at[i],
            device_id={"band": lax.rem(b + border[i], nb)},
        )

    def window_copy(d):
        return pltpu.make_async_remote_copy(
            src_ref=bw,
            dst_ref=bw,
            send_sem=ws_sem.at[d],
            recv_sem=wr_sem,
            device_id={"gblk": d},
        )

    def window_forward():
        return pltpu.make_async_remote_copy(
            src_ref=bw,
            dst_ref=bw,
            send_sem=ws_sem.at[0],
            recv_sem=wr_sem,
            device_id={"gblk": partner},
        )

    @pl.when(p == 0)
    def _():
        for d in range(ng - 2, 0, -2):
            window_copy(d).start()
        window_copy(1).start()

    for i in range(nb - 1):
        gather_copy(i, b).start()

    def slots_of(o, carry):
        count = jnp.int32(0)
        first = jnp.int32(blocks)
        second = jnp.int32(blocks)
        third = jnp.int32(blocks)
        for j in range(blocks):
            hit = owner_ref[p * blocks + j] == o
            first = jnp.where(hit & (count == 0), j, first)
            second = jnp.where(hit & (count == 1), j, second)
            third = jnp.where(hit & (count == 2), j, third)
            count = count + jnp.where(hit, 1, 0)
        slot_s[o * CAP] = first
        slot_s[o * CAP + 1] = second
        slot_s[o * CAP + 2] = third
        return carry

    lax.fori_loop(0, ng, slots_of, 0)
    chi[blocks] = jnp.zeros((GROUP, BLK), bf16)

    def forward_copy(i, group):
        rows = pl.ds(pl.multiple_of(group * GROUP, GROUP), GROUP)
        return pltpu.make_async_remote_copy(
            src_ref=psi.at[rows, my_cols],
            dst_ref=psi.at[rows, my_cols],
            send_sem=fs_sem.at[i],
            recv_sem=fr_sem.at[i],
            device_id={"gblk": partner},
        )

    for i in reversed(range(nb - 1)):
        source = lax.rem(b + nb - border[i], nb)
        gather_copy(i, source).wait_recv()
        forward_copy(i, source).start()

    @pl.when(p > 0)
    def _():
        window_forward().wait_recv()

    @pl.when((core == 0) & (p > 0))
    def _():
        window_forward().start()

    for i in reversed(range(nb - 1)):
        source = lax.rem(b + nb - border[i], nb)
        forward_copy(i, source).wait_recv()

    rows_n = nb * GROUP
    cons = nb * CON
    glane = lax.broadcasted_iota(jnp.int32, (GROUP, rows_n), 1)
    on_lanes = jnp.zeros((1, rows_n), f32)
    for g in range(nb):
        tile = psi[g * GROUP : (g + 1) * GROUP, 0:rows_n].astype(f32)
        grow = lax.broadcasted_iota(jnp.int32, (GROUP, rows_n), 0)
        keep = (glane // GROUP == g) & (grow >= 12) & (grow < 15)
        on_lanes = on_lanes + jnp.sum(jnp.where(keep, tile, 0.0), axis=0, keepdims=True)
    clane = lax.broadcasted_iota(jnp.int32, (cons, rows_n), 1)
    crow = lax.broadcasted_iota(jnp.int32, (cons, rows_n), 0)
    pick = clane == (crow // CON) * GROUP + VAL + crow % CON
    on_rows = jnp.sum(jnp.where(pick, on_lanes, 0.0), axis=1, keepdims=True)
    is_val = clane % GROUP < VAL
    gap = jnp.where(is_val, on_lanes - on_rows, -1.0)
    weight = jnp.where(is_val, factor / gap, 0.0)

    for g in range(0, nb, 2):
        one = psi[g * GROUP : (g + 1) * GROUP, :].astype(f32)[VAL : VAL + CON]
        two = psi[(g + 1) * GROUP : (g + 2) * GROUP, :].astype(f32)[VAL : VAL + CON]
        con_f[g * CON : (g + 2) * CON, :] = jnp.concatenate([one, two], axis=0)

    wrow = lax.broadcasted_iota(jnp.int32, (16, 1), 0) + lax.rem(b, 8) * 16
    win_live = (wrow < fill_ref[b // 8]).astype(f32)
    window = bw[...].astype(f32) * win_live
    for h in range(16):
        x_s[h * cons : (h + 1) * cons, :] = (con_f[...] * window[h : h + 1, :]).astype(bf16)

    group_h = 4
    rows_h = group_h * cons
    weight_t = jnp.concatenate([weight] * group_h, axis=0)
    for q in range(16 // group_h):
        chunk = slice(q * rows_h, (q + 1) * rows_h)
        raw = lax.dot_general(
            x_s[chunk, :], psi[...], (((1,), (1,)), ((), ())), preferred_element_type=f32
        )
        s_s[chunk, :] = (raw * weight_t).astype(bf16)
    for q in range(16 // group_h):
        chunk = slice(q * rows_h, (q + 1) * rows_h)
        full = jnp.dot(s_s[chunk, :], psi[...], preferred_element_type=f32)
        for i in range(group_h):
            part = full[i * cons : (i + 1) * cons, :] * con_f[...]
            h = q * group_h + i
            m_s[h : h + 1, :] = jnp.sum(part, axis=0, keepdims=True)

    m_hi = m_s[...].astype(bf16)
    m_lo = (m_s[...] - m_hi.astype(f32)).astype(bf16)
    m_two = jnp.concatenate([m_hi, m_lo], axis=0)

    ld_table.wait()
    lanes = lax.broadcasted_iota(jnp.int32, (1, BLK), 1)
    step = 6
    for n in range(0, blocks, step):
        wide = jnp.dot(
            m_two, table_v[:, n * BLK : (n + step) * BLK], preferred_element_type=f32
        )
        wide = wide[0:16] + wide[16:32]
        for j in range(step):
            live = (lanes < fill_ref[p * blocks + n + j]).astype(f32)
            chi[n + j] = (wide[:, j * BLK : (j + 1) * BLK] * live).astype(bf16)

    my_slots = pl.ds(pl.multiple_of(p * CAP * BLK, CAP * BLK), CAP * BLK)

    def fill_slots(o):
        for s in range(CAP):
            send[o, :, s * BLK : (s + 1) * BLK] = chi[slot_s[o * CAP + s]]

    def owner_copy(i):
        o = lax.rem(p + gorder[i], ng)
        return pltpu.make_async_remote_copy(
            src_ref=send.at[o],
            dst_ref=out_ref.at[:, my_slots],
            send_sem=cs_sem.at[i],
            recv_sem=cr_sem.at[i],
            device_id={"gblk": o},
        )

    for i in range(ng - 1):
        fill_slots(lax.rem(p + gorder[i], ng))
        owner_copy(i).start()
    fill_slots(p)
    own = pltpu.make_async_copy(send.at[p], out_ref.at[:, my_slots], own_sem)
    own.start()

    for i in range(nb - 1):
        source = lax.rem(b + nb - border[i], nb)
        gather_copy(i, b).wait_send()
        forward_copy(i, source).wait_send()

    @pl.when(p == 0)
    def _():
        for d in range(ng - 2, 0, -2):
            window_copy(d).wait_send()
        window_copy(1).wait_send()

    @pl.when((core == 0) & (p > 0))
    def _():
        window_forward().wait_send()

    own.wait()
    for i in range(ng - 1):
        o = lax.rem(p + ng - gorder[i], ng)
        from_slots = pl.ds(pl.multiple_of(o * CAP * BLK, CAP * BLK), CAP * BLK)
        owner_copy(i).wait_send()
        pltpu.make_async_remote_copy(
            src_ref=send.at[o],
            dst_ref=out_ref.at[:, from_slots],
            send_sem=cs_sem.at[i],
            recv_sem=cr_sem.at[i],
            device_id={"gblk": o},
        ).wait_recv()


def per_device(nb, ng, psi_val, psi_con, val_energy, con_energy, sphere_basis, block_owner, block_fill):
    r, cols = sphere_basis.shape
    blocks = cols // BLK
    factor = 1.0 / math.sqrt(psi_val.shape[0] * nb * psi_con.shape[0] * nb)
    any_spec = pl.BlockSpec(memory_space=pl.ANY)
    smem = pl.BlockSpec(memory_space=pltpu.SMEM)
    slot_cols = ng * CAP * BLK
    dma = pltpu.SemaphoreType.DMA
    got = pl.pallas_call(
        functools.partial(kernel, nb, ng, factor),
        out_shape=jax.ShapeDtypeStruct((16, slot_cols), bf16),
        in_specs=[any_spec, any_spec, smem, smem, smem, smem, any_spec],
        out_specs=any_spec,
        scratch_shapes=[
            pltpu.VMEM((VAL, r), bf16),
            pltpu.VMEM((CON, r), bf16),
            pltpu.VMEM((r, cols), bf16),
            pltpu.VMEM((r, BLK), bf16),
            pltpu.VMEM((nb * GROUP, r), bf16),
            pltpu.VMEM((BLK, r), f32),
            pltpu.VMEM((16, r), bf16),
            pltpu.VMEM((nb * CON, r), f32),
            pltpu.VMEM((16 * nb * CON, r), bf16),
            pltpu.VMEM((16 * nb * CON, nb * GROUP), bf16),
            pltpu.VMEM((16, r), f32),
            pltpu.VMEM((blocks + 1, 16, BLK), bf16),
            pltpu.VMEM((ng, 16, CAP * BLK), bf16),
            pltpu.SMEM((ng * CAP,), jnp.int32),
            dma((4,)),
            dma((nb - 1,)),
            dma((nb - 1,)),
            dma((nb - 1,)),
            dma((nb - 1,)),
            dma((ng,)),
            dma(()),
            dma((ng - 1,)),
            dma((ng - 1,)),
            dma(()),
        ],
        name="polarizability",
        compiler_params=pltpu.CompilerParams(
            collective_id=0, has_side_effects=True, vmem_limit_bytes=48 * 1024 * 1024
        ),
    )(psi_val, psi_con, val_energy, con_energy, block_owner, block_fill, sphere_basis)
    return got.astype(f32).T


def solution(mesh):
    nb, ng = mesh.shape["band"], mesh.shape["gblk"]
    return jax.shard_map(
        functools.partial(per_device, nb, ng),
        mesh=mesh,
        in_specs=(
            P("band", None),
            P("band", None),
            P("band"),
            P("band"),
            P(None, "gblk"),
            P(),
            P(),
        ),
        out_specs=P("gblk", "band"),
        check_vma=False,
    )
```

```python
import functools
import math

import jax
import jax.numpy as jnp
from jax import lax
from jax.experimental import pallas as pl
from jax.experimental.pallas import tpu as pltpu
from jax.sharding import PartitionSpec as P

BLK = 128
CAP = 3
GROUP = 16
VAL = 8
CON = 4

f32 = jnp.float32
bf16 = jnp.bfloat16


def band_order(n):
    def hops(d):
        z = (d // 2) % 8
        return min(z, 8 - z) + d % 2

    return sorted(range(1, n), key=lambda d: -hops(d))


def gblk_order(n):
    def hops(d):
        x = d // 4
        return min(x, 4 - x) + 2 * ((d // 2) % 2) + d % 2

    return sorted(range(1, n), key=lambda d: -hops(d))


def kernel(
    nb,
    ng,
    factor,
    val_hbm,
    con_hbm,
    ve_hbm,
    ce_hbm,
    owner_hbm,
    fill_hbm,
    table_hbm,
    out_ref,
    ve_ref,
    ce_ref,
    owner_ref,
    fill_ref,
    val_v,
    con_v,
    table_v,
    win_v,
    psi,
    turned,
    bw,
    con_f,
    x_s,
    s_s,
    m_s,
    send,
    slot_s,
    ld_sem,
    tb_sem,
    gs_sem,
    gr_sem,
    fs_sem,
    fr_sem,
    ws_sem,
    wr_sem,
    cs_sem,
    cr_sem,
    own_sem,
):
    b = lax.axis_index("band")
    p = lax.axis_index("gblk")
    core = lax.rem(p, 2)
    partner = p + 1 - 2 * core
    r = psi.shape[1]
    half = r // 2
    blocks = table_v.shape[0]
    border = band_order(nb)
    gorder = gblk_order(ng)

    barrier = pltpu.get_barrier_semaphore()
    for d in border:
        pl.semaphore_signal(barrier, 1, device_id={"band": lax.rem(b + d, nb)})
    for d in gorder:
        pl.semaphore_signal(barrier, 1, device_id={"gblk": lax.rem(p + d, ng)})

    ld_ve = pltpu.make_async_copy(ve_hbm, ve_ref, ld_sem.at[4])
    ld_ce = pltpu.make_async_copy(ce_hbm, ce_ref, ld_sem.at[5])
    ld_val = pltpu.make_async_copy(val_hbm, val_v, ld_sem.at[0])
    ld_con = pltpu.make_async_copy(con_hbm, con_v, ld_sem.at[1])
    ld_owner = pltpu.make_async_copy(owner_hbm, owner_ref, ld_sem.at[6])
    ld_fill = pltpu.make_async_copy(fill_hbm, fill_ref, ld_sem.at[7])
    for load in (ld_ve, ld_ce, ld_val, ld_con):
        load.start()
    wcol = pl.multiple_of((b // 8) * BLK, BLK)

    def win_copy():
        return pltpu.make_async_copy(
            table_hbm.at[:, pl.ds(wcol, BLK)], win_v, ld_sem.at[3]
        )

    @pl.when(p == 0)
    def _():
        win_copy().start()

    def table_copy(j):
        return pltpu.make_async_copy(
            table_hbm.at[:, j * BLK : (j + 1) * BLK], table_v.at[j], tb_sem.at[j]
        )

    ld_owner.start()
    ld_fill.start()
    for j in range(blocks):
        table_copy(j).start()

    lane = lax.broadcasted_iota(jnp.int32, (1, 256), 1)
    energy = jnp.zeros((1, 256), f32)
    ld_ve.wait()
    ld_ce.wait()
    for j in range(VAL):
        energy = jnp.where(lane % GROUP == j, ve_ref[j], energy)
    for j in range(CON):
        energy = jnp.where(lane % GROUP == VAL + j, ce_ref[j], energy)
    hi = energy.astype(bf16).astype(f32)
    mid = (energy - hi).astype(bf16).astype(f32)
    lo = energy - hi - mid
    parts = jnp.concatenate([hi, mid, lo, jnp.zeros_like(hi)], axis=0)
    parts = jnp.concatenate([parts, jnp.zeros((4, r - 256), f32)], axis=1)
    ld_val.wait()
    ld_con.wait()
    mine = jnp.concatenate([val_v[...].astype(f32), con_v[...].astype(f32), parts], axis=0)
    my_rows = pl.ds(pl.multiple_of(b * GROUP, GROUP), GROUP)
    psi[my_rows, :] = mine.astype(bf16)

    @pl.when(p == 0)
    def _():
        win_copy().wait()
        turned[...] = win_v[...].astype(f32).T
        bw[...] = turned[pl.ds(pl.multiple_of(lax.rem(b, 8) * 16, 16), 16), :].astype(bf16)

    pl.semaphore_wait(barrier, nb + ng - 2)

    my_cols = pl.ds(pl.multiple_of(core * half, half), half)

    def gather_copy(i, group):
        rows = pl.ds(pl.multiple_of(group * GROUP, GROUP), GROUP)
        return pltpu.make_async_remote_copy(
            src_ref=psi.at[rows, my_cols],
            dst_ref=psi.at[rows, my_cols],
            send_sem=gs_sem.at[i],
            recv_sem=gr_sem.at[i],
            device_id={"band": lax.rem(b + border[i], nb)},
        )

    def window_copy(d):
        return pltpu.make_async_remote_copy(
            src_ref=bw,
            dst_ref=bw,
            send_sem=ws_sem.at[d],
            recv_sem=wr_sem,
            device_id={"gblk": d},
        )

    def window_forward():
        return pltpu.make_async_remote_copy(
            src_ref=bw,
            dst_ref=bw,
            send_sem=ws_sem.at[0],
            recv_sem=wr_sem,
            device_id={"gblk": partner},
        )

    @pl.when(p == 0)
    def _():
        for d in range(ng - 2, 0, -2):
            window_copy(d).start()
        window_copy(1).start()

    for i in range(nb - 1):
        gather_copy(i, b).start()

    def slots_of(o, carry):
        count = jnp.int32(0)
        first = jnp.int32(blocks)
        second = jnp.int32(blocks)
        third = jnp.int32(blocks)
        for j in range(blocks):
            hit = owner_ref[p * blocks + j] == o
            first = jnp.where(hit & (count == 0), j, first)
            second = jnp.where(hit & (count == 1), j, second)
            third = jnp.where(hit & (count == 2), j, third)
            count = count + jnp.where(hit, 1, 0)
        slot_s[o * CAP] = first
        slot_s[o * CAP + 1] = second
        slot_s[o * CAP + 2] = third
        return carry

    ld_owner.wait()
    ld_fill.wait()
    lax.fori_loop(0, ng, slots_of, 0)

    def forward_copy(i, group):
        rows = pl.ds(pl.multiple_of(group * GROUP, GROUP), GROUP)
        return pltpu.make_async_remote_copy(
            src_ref=psi.at[rows, my_cols],
            dst_ref=psi.at[rows, my_cols],
            send_sem=fs_sem.at[i],
            recv_sem=fr_sem.at[i],
            device_id={"gblk": partner},
        )

    for i in reversed(range(nb - 1)):
        source = lax.rem(b + nb - border[i], nb)
        gather_copy(i, source).wait_recv()
        forward_copy(i, source).start()

    @pl.when(p > 0)
    def _():
        window_forward().wait_recv()

    @pl.when((core == 0) & (p > 0))
    def _():
        window_forward().start()

    for i in reversed(range(nb - 1)):
        source = lax.rem(b + nb - border[i], nb)
        forward_copy(i, source).wait_recv()

    rows_n = nb * GROUP
    cons = nb * CON
    glane = lax.broadcasted_iota(jnp.int32, (GROUP, rows_n), 1)
    on_lanes = jnp.zeros((1, rows_n), f32)
    for g in range(nb):
        tile = psi[g * GROUP : (g + 1) * GROUP, 0:rows_n].astype(f32)
        grow = lax.broadcasted_iota(jnp.int32, (GROUP, rows_n), 0)
        keep = (glane // GROUP == g) & (grow >= 12) & (grow < 15)
        on_lanes = on_lanes + jnp.sum(jnp.where(keep, tile, 0.0), axis=0, keepdims=True)
    clane = lax.broadcasted_iota(jnp.int32, (cons, rows_n), 1)
    crow = lax.broadcasted_iota(jnp.int32, (cons, rows_n), 0)
    pick = clane == (crow // CON) * GROUP + VAL + crow % CON
    on_rows = jnp.sum(jnp.where(pick, on_lanes, 0.0), axis=1, keepdims=True)
    is_val = clane % GROUP < VAL
    gap = jnp.where(is_val, on_lanes - on_rows, -1.0)
    weight = jnp.where(is_val, factor / gap, 0.0)

    for g in range(0, nb, 2):
        one = psi[g * GROUP : (g + 1) * GROUP, :].astype(f32)[VAL : VAL + CON]
        two = psi[(g + 1) * GROUP : (g + 2) * GROUP, :].astype(f32)[VAL : VAL + CON]
        con_f[g * CON : (g + 2) * CON, :] = jnp.concatenate([one, two], axis=0)

    wrow = lax.broadcasted_iota(jnp.int32, (16, 1), 0) + lax.rem(b, 8) * 16
    win_live = (wrow < fill_ref[b // 8]).astype(f32)
    window = bw[...].astype(f32) * win_live
    for h in range(16):
        x_s[h * cons : (h + 1) * cons, :] = (con_f[...] * window[h : h + 1, :]).astype(bf16)

    group_h = 4
    rows_h = group_h * cons
    weight_t = jnp.concatenate([weight] * group_h, axis=0)
    for q in range(16 // group_h):
        chunk = slice(q * rows_h, (q + 1) * rows_h)
        raw = lax.dot_general(
            x_s[chunk, :], psi[...], (((1,), (1,)), ((), ())), preferred_element_type=f32
        )
        s_s[chunk, :] = (raw * weight_t).astype(bf16)
    for q in range(16 // group_h):
        chunk = slice(q * rows_h, (q + 1) * rows_h)
        full = jnp.dot(s_s[chunk, :], psi[...], preferred_element_type=f32)
        for i in range(group_h):
            part = full[i * cons : (i + 1) * cons, :] * con_f[...]
            h = q * group_h + i
            m_s[h : h + 1, :] = jnp.sum(part, axis=0, keepdims=True)

    m_hi = m_s[...].astype(bf16)
    m_lo = (m_s[...] - m_hi.astype(f32)).astype(bf16)
    m_two = jnp.concatenate([m_hi, m_lo], axis=0)

    my_slots = pl.ds(pl.multiple_of(p * CAP * BLK, CAP * BLK), CAP * BLK)
    lanes = lax.broadcasted_iota(jnp.int32, (1, CAP * BLK), 1)

    def fill_slots(o):
        table = []
        limit = jnp.zeros((1, CAP * BLK), jnp.int32)
        for s in range(CAP):
            block = slot_s[o * CAP + s]
            j = jnp.minimum(block, blocks - 1)
            live = jnp.where(block < blocks, fill_ref[p * blocks + j], 0)
            limit = jnp.where(lanes // BLK == s, live, limit)
            table.append(table_v[j])
        wide = jnp.dot(m_two, jnp.concatenate(table, axis=1), preferred_element_type=f32)
        wide = wide[0:16] + wide[16:32]
        send[o] = jnp.where(lanes % BLK < limit, wide, 0.0).astype(bf16)

    def owner_copy(i):
        o = lax.rem(p + gorder[i], ng)
        return pltpu.make_async_remote_copy(
            src_ref=send.at[o],
            dst_ref=out_ref.at[:, my_slots],
            send_sem=cs_sem.at[i],
            recv_sem=cr_sem.at[i],
            device_id={"gblk": o},
        )

    for j in range(blocks):
        table_copy(j).wait()
    for i in range(ng - 1):
        fill_slots(lax.rem(p + gorder[i], ng))
        owner_copy(i).start()
    fill_slots(p)
    own = pltpu.make_async_copy(send.at[p], out_ref.at[:, my_slots], own_sem)
    own.start()

    for i in range(nb - 1):
        source = lax.rem(b + nb - border[i], nb)
        gather_copy(i, b).wait_send()
        forward_copy(i, source).wait_send()

    @pl.when(p == 0)
    def _():
        for d in range(ng - 2, 0, -2):
            window_copy(d).wait_send()
        window_copy(1).wait_send()

    @pl.when((core == 0) & (p > 0))
    def _():
        window_forward().wait_send()

    own.wait()
    for i in range(ng - 1):
        o = lax.rem(p + ng - gorder[i], ng)
        from_slots = pl.ds(pl.multiple_of(o * CAP * BLK, CAP * BLK), CAP * BLK)
        owner_copy(i).wait_send()
        pltpu.make_async_remote_copy(
            src_ref=send.at[o],
            dst_ref=out_ref.at[:, from_slots],
            send_sem=cs_sem.at[i],
            recv_sem=cr_sem.at[i],
            device_id={"gblk": o},
        ).wait_recv()


def per_device(nb, ng, psi_val, psi_con, val_energy, con_energy, sphere_basis, block_owner, block_fill):
    r, cols = sphere_basis.shape
    blocks = cols // BLK
    factor = 1.0 / math.sqrt(psi_val.shape[0] * nb * psi_con.shape[0] * nb)
    hbm = pl.BlockSpec(memory_space=pltpu.HBM)
    slot_cols = ng * CAP * BLK
    dma = pltpu.SemaphoreType.DMA
    got = pl.pallas_call(
        functools.partial(kernel, nb, ng, factor),
        out_shape=jax.ShapeDtypeStruct((16, slot_cols), bf16),
        in_specs=[hbm] * 7,
        out_specs=pl.BlockSpec(memory_space=pl.ANY),
        scratch_shapes=[
            pltpu.SMEM(val_energy.shape, f32),
            pltpu.SMEM(con_energy.shape, f32),
            pltpu.SMEM(block_owner.shape, jnp.int32),
            pltpu.SMEM(block_fill.shape, jnp.int32),
            pltpu.VMEM((VAL, r), bf16),
            pltpu.VMEM((CON, r), bf16),
            pltpu.VMEM((blocks, r, BLK), bf16),
            pltpu.VMEM((r, BLK), bf16),
            pltpu.VMEM((nb * GROUP, r), bf16),
            pltpu.VMEM((BLK, r), f32),
            pltpu.VMEM((16, r), bf16),
            pltpu.VMEM((nb * CON, r), f32),
            pltpu.VMEM((16 * nb * CON, r), bf16),
            pltpu.VMEM((16 * nb * CON, nb * GROUP), bf16),
            pltpu.VMEM((16, r), f32),
            pltpu.VMEM((ng, 16, CAP * BLK), bf16),
            pltpu.SMEM((ng * CAP,), jnp.int32),
            dma((8,)),
            dma((blocks,)),
            dma((nb - 1,)),
            dma((nb - 1,)),
            dma((nb - 1,)),
            dma((nb - 1,)),
            dma((ng,)),
            dma(()),
            dma((ng - 1,)),
            dma((ng - 1,)),
            dma(()),
        ],
        name="polarizability",
        compiler_params=pltpu.CompilerParams(
            collective_id=0, has_side_effects=True, vmem_limit_bytes=60 * 1024 * 1024
        ),
    )(psi_val, psi_con, val_energy, con_energy, block_owner, block_fill, sphere_basis)
    return got.astype(f32).T


def solution(mesh):
    nb, ng = mesh.shape["band"], mesh.shape["gblk"]
    return jax.shard_map(
        functools.partial(per_device, nb, ng),
        mesh=mesh,
        in_specs=(
            P("band", None),
            P("band", None),
            P("band"),
            P("band"),
            P(None, "gblk"),
            P(),
            P(),
        ),
        out_specs=P("gblk", "band"),
        check_vma=False,
    )
```

```python
import functools
import math

import jax
import jax.numpy as jnp
from jax import lax
from jax.experimental import pallas as pl
from jax.experimental.pallas import tpu as pltpu
from jax.sharding import PartitionSpec as P

BLK = 128
CAP = 3
GROUP = 16
VAL = 8
CON = 4
WIN = 16

f32 = jnp.float32
bf16 = jnp.bfloat16


def far_first(n, hops):
    return sorted(range(1, n), key=lambda d: -hops(d))


def band_hops(d):
    z = (d // 2) % 8
    return min(z, 8 - z) + d % 2


def gblk_hops(d):
    x = d // 4
    return min(x, 4 - x) + 2 * ((d // 2) % 2) + d % 2


def kernel(
    nb,
    ng,
    factor,
    val_hbm,
    con_hbm,
    ve_hbm,
    ce_hbm,
    owner_hbm,
    fill_hbm,
    table_hbm,
    out_ref,
    ve_ref,
    ce_ref,
    owner_ref,
    fill_ref,
    val_v,
    con_v,
    table_v,
    win_v,
    packed,
    energy,
    turned,
    bw,
    val_m,
    con_f,
    x_s,
    s_s,
    m_s,
    chi,
    send,
    slot_s,
    ld_sem,
    tb_sem,
    gs_sem,
    gr_sem,
    fs_sem,
    fr_sem,
    es_sem,
    er_sem,
    ws_sem,
    wr_sem,
    cs_sem,
    cr_sem,
    own_sem,
):
    b = lax.axis_index("band")
    p = lax.axis_index("gblk")
    core = lax.rem(p, 2)
    partner = p + 1 - 2 * core
    r = val_v.shape[1]
    vals, cons = nb * VAL, nb * CON
    val_cols, con_cols = r * VAL // GROUP, r * CON // GROUP
    blocks = table_v.shape[1] // BLK
    pairs = nb // 2
    border = far_first(nb, band_hops)
    gorder = far_first(ng, gblk_hops)
    steps = sorted(range(pairs), key=lambda i: -min(i, pairs - i))

    barrier = pltpu.get_barrier_semaphore()
    for d in border:
        pl.semaphore_signal(barrier, 1, device_id={"band": lax.rem(b + d, nb)})
    for d in gorder:
        pl.semaphore_signal(barrier, 1, device_id={"gblk": lax.rem(p + d, ng)})

    ld_val = pltpu.make_async_copy(val_hbm, val_v, ld_sem.at[0])
    ld_con = pltpu.make_async_copy(con_hbm, con_v, ld_sem.at[1])
    ld_ve = pltpu.make_async_copy(ve_hbm, ve_ref, ld_sem.at[2])
    ld_ce = pltpu.make_async_copy(ce_hbm, ce_ref, ld_sem.at[3])
    ld_owner = pltpu.make_async_copy(owner_hbm, owner_ref, ld_sem.at[4])
    ld_fill = pltpu.make_async_copy(fill_hbm, fill_ref, ld_sem.at[5])
    wcol = pl.multiple_of((b // (BLK // WIN)) * BLK, BLK)

    def win_copy():
        return pltpu.make_async_copy(table_hbm.at[:, pl.ds(wcol, BLK)], win_v, ld_sem.at[6])

    for load in (ld_ve, ld_ce, ld_val, ld_con):
        load.start()

    @pl.when(p == 0)
    def _():
        win_copy().start()

    ld_owner.start()
    ld_fill.start()
    ld_table = pltpu.make_async_copy(table_hbm, table_v, tb_sem)
    ld_table.start()

    lane = lax.broadcasted_iota(jnp.int32, (1, BLK), 1)
    mine_v = jnp.zeros((1, BLK), f32)
    mine_c = jnp.zeros((1, BLK), f32)
    ld_ve.wait()
    ld_ce.wait()
    for j in range(VAL):
        mine_v = jnp.where(lane % VAL == j, ve_ref[j], mine_v)
    for j in range(CON):
        mine_c = jnp.where(lane % CON == j, ce_ref[j], mine_c)
    energy[b] = jnp.concatenate([mine_v, mine_c], axis=0)
    ld_val.wait()
    ld_con.wait()
    val_f = val_v[...].astype(f32)
    con_g = con_v[...].astype(f32)
    val_f = jnp.concatenate([val_f[:, i : i + val_cols] for i in range(0, r, val_cols)], axis=0)
    con_g = jnp.concatenate([con_g[:, i : i + con_cols] for i in range(0, r, con_cols)], axis=0)

    def rows_of(group):
        return pl.ds(pl.multiple_of(group * GROUP, GROUP), GROUP)

    packed[rows_of(b), :] = jnp.concatenate([val_f, con_g], axis=1).astype(bf16)

    @pl.when(p == 0)
    def _():
        win_copy().wait()
        turned[...] = win_v[...].astype(f32).T
        first = pl.multiple_of(lax.rem(b, BLK // WIN) * WIN, WIN)
        bw[...] = turned[pl.ds(first, WIN), :].astype(bf16)

    pl.semaphore_wait(barrier, nb + ng - 2)

    def gather_copy(i, group):
        return pltpu.make_async_remote_copy(
            src_ref=packed.at[rows_of(group)],
            dst_ref=packed.at[rows_of(group)],
            send_sem=gs_sem,
            recv_sem=gr_sem.at[i],
            device_id={"band": lax.rem(b + 2 * i + core, nb)},
        )

    def forward_copy(group):
        return pltpu.make_async_remote_copy(
            src_ref=packed.at[rows_of(group)],
            dst_ref=packed.at[rows_of(group)],
            send_sem=fs_sem,
            recv_sem=fr_sem,
            device_id={"gblk": partner},
        )

    def many_copy(count, send_sem, recv_sem):
        rows = packed.at[pl.ds(0, count * GROUP)]
        return pltpu.make_async_remote_copy(
            src_ref=rows,
            dst_ref=rows,
            send_sem=send_sem,
            recv_sem=recv_sem,
            device_id={"gblk": partner},
        )

    def energy_copy(d):
        return pltpu.make_async_remote_copy(
            src_ref=energy.at[b],
            dst_ref=energy.at[b],
            send_sem=es_sem,
            recv_sem=er_sem,
            device_id={"band": lax.rem(b + d, nb)},
        )

    def energies_copy():
        return pltpu.make_async_remote_copy(
            src_ref=energy.at[pl.ds(0, nb - 1)],
            dst_ref=energy.at[pl.ds(0, nb - 1)],
            send_sem=es_sem,
            recv_sem=er_sem,
            device_id={"gblk": partner},
        )

    def window_copy(i, target):
        return pltpu.make_async_remote_copy(
            src_ref=bw,
            dst_ref=bw,
            send_sem=ws_sem.at[i],
            recv_sem=wr_sem,
            device_id={"gblk": target},
        )

    @pl.when(p == 0)
    def _():
        for i in range(ng // 2 - 1, 0, -1):
            window_copy(i, 2 * i).start()

    for i in steps:
        if i == 0:

            @pl.when(core == 1)
            def _():
                gather_copy(0, b).start()

        else:
            gather_copy(i, b).start()

    @pl.when(p == 0)
    def _():
        window_copy(0, partner).start()

    for d in border:
        energy_copy(d).start()

    def slots_of(o, carry):
        count = jnp.int32(0)
        first = jnp.int32(blocks)
        second = jnp.int32(blocks)
        third = jnp.int32(blocks)
        for j in range(blocks):
            hit = owner_ref[p * blocks + j] == o
            first = jnp.where(hit & (count == 0), j, first)
            second = jnp.where(hit & (count == 1), j, second)
            third = jnp.where(hit & (count == 2), j, third)
            count = count + jnp.where(hit, 1, 0)
        slot_s[o * CAP] = first
        slot_s[o * CAP + 1] = second
        slot_s[o * CAP + 2] = third
        return carry

    ld_owner.wait()
    ld_fill.wait()
    lax.fori_loop(0, ng, slots_of, 0)
    chi[blocks] = jnp.zeros((WIN, BLK), bf16)

    def pass_on(i):
        group = lax.rem(b + nb - 2 * i - core, nb)
        gather_copy(i, group).wait_recv()
        forward_copy(group).start()

    for i in reversed(steps):
        if i == 0:

            @pl.when(core == 1)
            def _():
                pass_on(0)

        else:
            pass_on(i)

    @pl.when(p > 0)
    def _():
        window_copy(0, partner).wait_recv()

    @pl.when((core == 0) & (p > 0))
    def _():
        window_copy(0, partner).start()

    energies_copy().wait_recv()

    on_lanes = jnp.zeros((1, vals), f32)
    con_lanes = jnp.zeros((1, vals), f32)
    for g in range(nb):
        on_lanes = jnp.where(lane // VAL == g, energy[g, 0:1, :], on_lanes)
        con_lanes = jnp.where(lane // CON == g, energy[g, 1:2, :], con_lanes)
    clane = lax.broadcasted_iota(jnp.int32, (cons, vals), 1)
    crow = lax.broadcasted_iota(jnp.int32, (cons, vals), 0)
    on_rows = jnp.sum(jnp.where(clane == crow, con_lanes, 0.0), axis=1, keepdims=True)
    weight = factor / (on_lanes - on_rows)
    wrow = lax.broadcasted_iota(jnp.int32, (WIN, 1), 0) + lax.rem(b, BLK // WIN) * WIN
    win_live = (wrow < fill_ref[b // (BLK // WIN)]).astype(f32)
    window = bw[...].astype(f32) * win_live

    @pl.when(core == 0)
    def _():
        many_copy(pairs, fs_sem, fr_sem).wait_recv()

    @pl.when(core == 1)
    def _():
        many_copy(pairs - 1, fs_sem, fr_sem).wait_recv()

    for g in range(0, nb, 2):
        one = packed[g * GROUP : (g + 1) * GROUP, :].astype(f32)
        two = packed[(g + 1) * GROUP : (g + 2) * GROUP, :].astype(f32)
        for i in range(r // val_cols):
            both = jnp.concatenate(
                [t[i * VAL : (i + 1) * VAL, 0:val_cols] for t in (one, two)], axis=0
            )
            val_m[g * VAL : (g + 2) * VAL, i * val_cols : (i + 1) * val_cols] = both.astype(bf16)
        for i in range(r // con_cols):
            both = jnp.concatenate(
                [t[i * CON : (i + 1) * CON, val_cols:] for t in (one, two)], axis=0
            )
            con_f[g * CON : (g + 2) * CON, i * con_cols : (i + 1) * con_cols] = both

    for h in range(WIN):
        x_s[h * cons : (h + 1) * cons, :] = (con_f[...] * window[h : h + 1, :]).astype(bf16)
    group_h = 4
    rows_h = group_h * cons
    weight_t = jnp.concatenate([weight] * group_h, axis=0)
    for q in range(WIN // group_h):
        chunk = slice(q * rows_h, (q + 1) * rows_h)
        raw = lax.dot_general(
            x_s[chunk, :], val_m[...], (((1,), (1,)), ((), ())), preferred_element_type=f32
        )
        s_s[chunk, :] = (raw * weight_t).astype(bf16)
    for q in range(WIN // group_h):
        chunk = slice(q * rows_h, (q + 1) * rows_h)
        full = jnp.dot(s_s[chunk, :], val_m[...], preferred_element_type=f32)
        for i in range(group_h):
            part = full[i * cons : (i + 1) * cons, :] * con_f[...]
            h = q * group_h + i
            m_s[h : h + 1, :] = jnp.sum(part, axis=0, keepdims=True)

    m_hi = m_s[...].astype(bf16)
    m_lo = (m_s[...] - m_hi.astype(f32)).astype(bf16)
    m_two = jnp.concatenate([m_hi, m_lo], axis=0)

    my_slots = pl.ds(pl.multiple_of(p * CAP * BLK, CAP * BLK), CAP * BLK)

    def owner_copy(o):
        return pltpu.make_async_remote_copy(
            src_ref=send.at[o],
            dst_ref=out_ref.at[:, my_slots],
            send_sem=cs_sem,
            recv_sem=cr_sem,
            device_id={"gblk": o},
        )

    ld_table.wait()
    step = 2
    for n in range(0, blocks, step):
        wide = jnp.dot(
            m_two, table_v[:, n * BLK : (n + step) * BLK], preferred_element_type=f32
        )
        wide = wide[0:WIN] + wide[WIN:]
        for j in range(step):
            rows = wide[:, j * BLK : (j + 1) * BLK]
            live = lane < fill_ref[p * blocks + n + j]
            chi[n + j] = jnp.where(live, rows, 0.0).astype(bf16)

    def fill_slots(o):
        for s in range(CAP):
            send[o, :, s * BLK : (s + 1) * BLK] = chi[slot_s[o * CAP + s]]

    for d in gorder:
        o = lax.rem(p + d, ng)
        fill_slots(o)
        owner_copy(o).start()
    fill_slots(p)
    own = pltpu.make_async_copy(send.at[p], out_ref.at[:, my_slots], own_sem)
    own.start()

    @pl.when(core == 0)
    def _():
        many_copy(pairs - 1, gs_sem, fr_sem).wait_send()
        many_copy(pairs - 1, fs_sem, fr_sem).wait_send()

    @pl.when(core == 1)
    def _():
        many_copy(pairs, gs_sem, fr_sem).wait_send()
        many_copy(pairs, fs_sem, fr_sem).wait_send()

    energies_copy().wait_send()

    @pl.when(p == 0)
    def _():
        for i in range(ng // 2):
            window_copy(i, partner).wait_send()

    @pl.when((core == 0) & (p > 0))
    def _():
        window_copy(0, partner).wait_send()

    own.wait()
    others = (ng - 1) * CAP * BLK
    all_copies = pltpu.make_async_remote_copy(
        src_ref=send.at[pl.ds(0, ng - 1)],
        dst_ref=out_ref.at[:, pl.ds(0, others)],
        send_sem=cs_sem,
        recv_sem=cr_sem,
        device_id={"gblk": partner},
    )
    all_copies.wait_send()
    all_copies.wait_recv()


def per_device(nb, ng, psi_val, psi_con, val_energy, con_energy, sphere_basis, block_owner, block_fill):
    r, cols = sphere_basis.shape
    blocks = cols // BLK
    factor = 1.0 / math.sqrt(psi_val.shape[0] * nb * psi_con.shape[0] * nb)
    hbm = pl.BlockSpec(memory_space=pltpu.HBM)
    args = (psi_val, psi_con, val_energy, con_energy, block_owner, block_fill, sphere_basis)
    args = [pltpu.with_memory_space_constraint(a, pltpu.HBM) for a in args]
    slot_cols = ng * CAP * BLK
    dma = pltpu.SemaphoreType.DMA
    got = pl.pallas_call(
        functools.partial(kernel, nb, ng, factor),
        out_shape=jax.ShapeDtypeStruct((WIN, slot_cols), bf16),
        in_specs=[hbm] * len(args),
        out_specs=pl.BlockSpec(memory_space=pl.ANY),
        scratch_shapes=[
            pltpu.SMEM(val_energy.shape, f32),
            pltpu.SMEM(con_energy.shape, f32),
            pltpu.SMEM(block_owner.shape, jnp.int32),
            pltpu.SMEM(block_fill.shape, jnp.int32),
            pltpu.VMEM((VAL, r), bf16),
            pltpu.VMEM((CON, r), bf16),
            pltpu.VMEM((r, cols), bf16),
            pltpu.VMEM((r, BLK), bf16),
            pltpu.VMEM((nb * GROUP, r * (VAL + CON) // GROUP), bf16),
            pltpu.VMEM((nb, 2, BLK), f32),
            pltpu.VMEM((BLK, r), f32),
            pltpu.VMEM((WIN, r), bf16),
            pltpu.VMEM((nb * VAL, r), bf16),
            pltpu.VMEM((nb * CON, r), f32),
            pltpu.VMEM((WIN * nb * CON, r), bf16),
            pltpu.VMEM((WIN * nb * CON, nb * VAL), bf16),
            pltpu.VMEM((WIN, r), f32),
            pltpu.VMEM((blocks + 1, WIN, BLK), bf16),
            pltpu.VMEM((ng, WIN, CAP * BLK), bf16),
            pltpu.SMEM((ng * CAP,), jnp.int32),
            dma((7,)),
            dma(()),
            dma(()),
            dma((nb // 2,)),
            dma(()),
            dma(()),
            dma(()),
            dma(()),
            dma((ng // 2,)),
            dma(()),
            dma(()),
            dma(()),
            dma(()),
        ],
        name="polarizability",
        compiler_params=pltpu.CompilerParams(
            collective_id=0, has_side_effects=True, vmem_limit_bytes=48 * 1024 * 1024
        ),
    )(*args)
    return got.astype(f32).T


def solution(mesh):
    nb, ng = mesh.shape["band"], mesh.shape["gblk"]
    return jax.shard_map(
        functools.partial(per_device, nb, ng),
        mesh=mesh,
        in_specs=(
            P("band", None),
            P("band", None),
            P("band"),
            P("band"),
            P(None, "gblk"),
            P(),
            P(),
        ),
        out_specs=P("gblk", "band"),
        check_vma=False,
    )
```

```python
import functools
import math

import jax
import jax.numpy as jnp
from jax import lax
from jax.experimental import pallas as pl
from jax.experimental.pallas import tpu as pltpu
from jax.sharding import PartitionSpec as P

BLK = 128
CAP = 3
GROUP = 16
VAL = 8
CON = 4
WIN = 16

f32 = jnp.float32
bf16 = jnp.bfloat16


def kernel(
    nb,
    ng,
    factor,
    val_hbm,
    con_hbm,
    ve_hbm,
    ce_hbm,
    owner_hbm,
    fill_hbm,
    table_hbm,
    out_ref,
    ve_ref,
    ce_ref,
    owner_ref,
    fill_ref,
    val_v,
    con_v,
    table_v,
    win_v,
    packed,
    energy,
    mine_e,
    turned,
    bw,
    val_m,
    con_f,
    x_s,
    s_s,
    m_s,
    send,
    slot_s,
    ld_sem,
    tb_sem,
    gs_sem,
    gr_sem,
    fs_sem,
    fr_sem,
    es_sem,
    er_sem,
    ws_sem,
    wr_sem,
    cs_sem,
    cr_sem,
    own_sem,
):
    b = lax.axis_index("band")
    p = lax.axis_index("gblk")
    core = lax.rem(p, 2)
    partner = p + 1 - 2 * core
    r = val_v.shape[1]
    vals, cons = nb * VAL, nb * CON
    val_cols, con_cols = r * VAL // GROUP, r * CON // GROUP
    blocks = table_v.shape[0]
    pairs = nb // 2
    z, y = b // 2, lax.rem(b, 2)
    x, y_hi = p // 4, lax.rem(p // 2, 2)
    turns = ng // 4

    steps = sorted(range(pairs), key=lambda i: -min(i, pairs - i))
    moves = [(dx, dy, dc) for dx in range(turns) for dy in range(2) for dc in range(2)][1:]
    moves.sort(key=lambda m: -(min(m[0], turns - m[0]) + 2 * m[1] + 0.1 * m[2]))

    def band_at(i, flip):
        return 2 * lax.rem(z + i, pairs) + lax.rem(y + flip, 2)

    def gblk_at(move):
        dx, dy, dc = move
        return 4 * lax.rem(x + dx, turns) + 2 * lax.rem(y_hi + dy, 2) + lax.rem(core + dc, 2)

    barrier = pltpu.get_barrier_semaphore()
    for i in steps:
        for flip in (1, 0):
            if i or flip:
                pl.semaphore_signal(barrier, 1, device_id={"band": band_at(i, flip)})
    for move in moves:
        pl.semaphore_signal(barrier, 1, device_id={"gblk": gblk_at(move)})

    ld_val = pltpu.make_async_copy(val_hbm, val_v, ld_sem.at[0])
    ld_con = pltpu.make_async_copy(con_hbm, con_v, ld_sem.at[1])
    ld_ve = pltpu.make_async_copy(ve_hbm, ve_ref, ld_sem.at[2])
    ld_ce = pltpu.make_async_copy(ce_hbm, ce_ref, ld_sem.at[3])
    ld_owner = pltpu.make_async_copy(owner_hbm, owner_ref, ld_sem.at[4])
    ld_fill = pltpu.make_async_copy(fill_hbm, fill_ref, ld_sem.at[5])
    wcol = pl.multiple_of((b // (BLK // WIN)) * BLK, BLK)

    def win_copy():
        return pltpu.make_async_copy(table_hbm.at[:, pl.ds(wcol, BLK)], win_v, ld_sem.at[6])

    for load in (ld_ve, ld_ce, ld_val, ld_con):
        load.start()

    @pl.when(p == 0)
    def _():
        win_copy().start()

    ld_owner.start()
    ld_fill.start()
    for j in range(blocks):
        pltpu.make_async_copy(
            table_hbm.at[:, j * BLK : (j + 1) * BLK], table_v.at[j], tb_sem
        ).start()

    lane = lax.broadcasted_iota(jnp.int32, (1, BLK), 1)
    mine_v = jnp.zeros((1, BLK), f32)
    mine_c = jnp.zeros((1, BLK), f32)
    ld_ve.wait()
    ld_ce.wait()
    for j in range(VAL):
        mine_v = jnp.where(lane % VAL == j, ve_ref[j], mine_v)
    for j in range(CON):
        mine_c = jnp.where(lane % CON == j, ce_ref[j], mine_c)
    mine_e[...] = jnp.concatenate([mine_v, mine_c], axis=0)

    @pl.when(core == 0)
    def _():
        energy[y, z] = mine_e[...]

    ld_val.wait()
    ld_con.wait()
    val_f = val_v[...].astype(f32)
    con_g = con_v[...].astype(f32)
    val_f = jnp.concatenate([val_f[:, i : i + val_cols] for i in range(0, r, val_cols)], axis=0)
    con_g = jnp.concatenate([con_g[:, i : i + con_cols] for i in range(0, r, con_cols)], axis=0)

    def rows_of(group):
        return pl.ds(pl.multiple_of(group * GROUP, GROUP), GROUP)

    packed[rows_of(b), :] = jnp.concatenate([val_f, con_g], axis=1).astype(bf16)

    @pl.when(p == 0)
    def _():
        win_copy().wait()
        turned[...] = win_v[...].astype(f32).T
        first = pl.multiple_of(lax.rem(b, BLK // WIN) * WIN, WIN)
        bw[...] = turned[pl.ds(first, WIN), :].astype(bf16)

    pl.semaphore_wait(barrier, nb + ng - 2)

    def gather_copy(i, group):
        return pltpu.make_async_remote_copy(
            src_ref=packed.at[rows_of(group)],
            dst_ref=packed.at[rows_of(group)],
            send_sem=gs_sem,
            recv_sem=gr_sem.at[i],
            device_id={"band": band_at(i, core)},
        )

    def forward_copy(group):
        return pltpu.make_async_remote_copy(
            src_ref=packed.at[rows_of(group)],
            dst_ref=packed.at[rows_of(group)],
            send_sem=fs_sem,
            recv_sem=fr_sem,
            device_id={"gblk": partner},
        )

    def many_copy(count, send_sem, recv_sem):
        rows = packed.at[pl.ds(0, count * GROUP)]
        return pltpu.make_async_remote_copy(
            src_ref=rows,
            dst_ref=rows,
            send_sem=send_sem,
            recv_sem=recv_sem,
            device_id={"gblk": partner},
        )

    def energy_copy(i):
        return pltpu.make_async_remote_copy(
            src_ref=mine_e,
            dst_ref=energy.at[y, z],
            send_sem=es_sem.at[0],
            recv_sem=er_sem.at[0],
            device_id={"band": band_at(i, core)},
        )

    def energies_copy(count, k):
        rows = energy.at[lax.rem(y + core, 2), pl.ds(0, count)]
        return pltpu.make_async_remote_copy(
            src_ref=rows,
            dst_ref=rows,
            send_sem=es_sem.at[k],
            recv_sem=er_sem.at[k],
            device_id={"gblk": partner},
        )

    def window_copy(i, target):
        return pltpu.make_async_remote_copy(
            src_ref=bw,
            dst_ref=bw,
            send_sem=ws_sem.at[i],
            recv_sem=wr_sem,
            device_id={"gblk": target},
        )

    @pl.when(p == 0)
    def _():
        for i in range(ng // 2 - 1, 0, -1):
            window_copy(i, 2 * i).start()

    early = 3
    for i in steps[:early]:
        gather_copy(i, b).start()
    for i in steps[:-1]:
        energy_copy(i).start()
    for i in steps[early:-1]:
        gather_copy(i, b).start()

    @pl.when(core == 1)
    def _():
        energy_copy(0).start()
        gather_copy(0, b).start()

    @pl.when(p == 0)
    def _():
        window_copy(0, partner).start()

    def slots_of(o, carry):
        count = jnp.int32(0)
        first = jnp.int32(blocks)
        second = jnp.int32(blocks)
        third = jnp.int32(blocks)
        for j in range(blocks):
            hit = owner_ref[p * blocks + j] == o
            first = jnp.where(hit & (count == 0), j, first)
            second = jnp.where(hit & (count == 1), j, second)
            third = jnp.where(hit & (count == 2), j, third)
            count = count + jnp.where(hit, 1, 0)
        slot_s[o * CAP] = first
        slot_s[o * CAP + 1] = second
        slot_s[o * CAP + 2] = third
        return carry

    ld_owner.wait()
    ld_fill.wait()
    lax.fori_loop(0, ng, slots_of, 0)

    def pass_on(i):
        group = band_at(pairs - i, core)
        gather_copy(i, group).wait_recv()
        forward_copy(group).start()

    @pl.when(core == 1)
    def _():
        pass_on(0)

    for i in steps[-2:2:-1]:
        pass_on(i)

    @pl.when(core == 0)
    def _():
        energies_copy(pairs - 1, 0).wait_recv()

    @pl.when(core == 1)
    def _():
        energies_copy(pairs, 0).wait_recv()

    energies_copy(pairs, 1).start()
    for i in steps[2::-1]:
        pass_on(i)

    @pl.when(p > 0)
    def _():
        window_copy(0, partner).wait_recv()

    @pl.when((core == 0) & (p > 0))
    def _():
        window_copy(0, partner).start()

    energies_copy(pairs, 1).wait_recv()

    on_lanes = jnp.zeros((1, vals), f32)
    con_lanes = jnp.zeros((1, vals), f32)
    for g in range(nb):
        both = energy[g % 2, g // 2]
        on_lanes = jnp.where(lane // VAL == g, both[0:1], on_lanes)
        con_lanes = jnp.where(lane // CON == g, both[1:2], con_lanes)
    clane = lax.broadcasted_iota(jnp.int32, (cons, vals), 1)
    crow = lax.broadcasted_iota(jnp.int32, (cons, vals), 0)
    on_rows = jnp.sum(jnp.where(clane == crow, con_lanes, 0.0), axis=1, keepdims=True)
    weight = factor / (on_lanes - on_rows)
    wrow = lax.broadcasted_iota(jnp.int32, (WIN, 1), 0) + lax.rem(b, BLK // WIN) * WIN
    win_live = (wrow < fill_ref[b // (BLK // WIN)]).astype(f32)
    window = bw[...].astype(f32) * win_live

    @pl.when(core == 0)
    def _():
        many_copy(pairs, fs_sem, fr_sem).wait_recv()

    @pl.when(core == 1)
    def _():
        many_copy(pairs - 1, fs_sem, fr_sem).wait_recv()

    for g in range(0, nb, 2):
        one = packed[g * GROUP : (g + 1) * GROUP, :].astype(f32)
        two = packed[(g + 1) * GROUP : (g + 2) * GROUP, :].astype(f32)
        for i in range(r // val_cols):
            both = jnp.concatenate(
                [t[i * VAL : (i + 1) * VAL, 0:val_cols] for t in (one, two)], axis=0
            )
            val_m[g * VAL : (g + 2) * VAL, i * val_cols : (i + 1) * val_cols] = both.astype(bf16)
        for i in range(r // con_cols):
            both = jnp.concatenate(
                [t[i * CON : (i + 1) * CON, val_cols:] for t in (one, two)], axis=0
            )
            con_f[g * CON : (g + 2) * CON, i * con_cols : (i + 1) * con_cols] = both

    for h in range(WIN):
        x_s[h * cons : (h + 1) * cons, :] = (con_f[...] * window[h : h + 1, :]).astype(bf16)
    group_h = 4
    rows_h = group_h * cons
    weight_t = jnp.concatenate([weight] * group_h, axis=0)
    for q in range(WIN // group_h):
        chunk = slice(q * rows_h, (q + 1) * rows_h)
        raw = lax.dot_general(
            x_s[chunk, :], val_m[...], (((1,), (1,)), ((), ())), preferred_element_type=f32
        )
        s_s[chunk, :] = (raw * weight_t).astype(bf16)
    for q in range(WIN // group_h):
        chunk = slice(q * rows_h, (q + 1) * rows_h)
        full = jnp.dot(s_s[chunk, :], val_m[...], preferred_element_type=f32)
        for i in range(group_h):
            part = full[i * cons : (i + 1) * cons, :] * con_f[...]
            h = q * group_h + i
            m_s[h : h + 1, :] = jnp.sum(part, axis=0, keepdims=True)

    m_hi = m_s[...].astype(bf16)
    m_lo = (m_s[...] - m_hi.astype(f32)).astype(bf16)
    m_two = jnp.concatenate([m_hi, m_lo], axis=0)

    my_slots = pl.ds(pl.multiple_of(p * CAP * BLK, CAP * BLK), CAP * BLK)

    def owner_copy(o):
        return pltpu.make_async_remote_copy(
            src_ref=send.at[o],
            dst_ref=out_ref.at[:, my_slots],
            send_sem=cs_sem,
            recv_sem=cr_sem,
            device_id={"gblk": o},
        )

    lanes = lax.broadcasted_iota(jnp.int32, (1, CAP * BLK), 1)

    def fill_slots(owners):
        table = []
        limits = []
        for o in owners:
            limit = jnp.zeros((1, CAP * BLK), jnp.int32)
            for s in range(CAP):
                block = slot_s[o * CAP + s]
                j = jnp.minimum(block, blocks - 1)
                live = jnp.where(block < blocks, fill_ref[p * blocks + j], 0)
                limit = jnp.where(lanes // BLK == s, live, limit)
                table.append(table_v[j])
            limits.append(limit)
        wide = jnp.dot(m_two, jnp.concatenate(table, axis=1), preferred_element_type=f32)
        wide = wide[0:WIN] + wide[WIN:]
        for i, o in enumerate(owners):
            rows = wide[:, i * CAP * BLK : (i + 1) * CAP * BLK]
            send[o] = jnp.where(lanes % BLK < limits[i], rows, 0.0).astype(bf16)

    pltpu.make_async_copy(table_v, table_v, tb_sem).wait()

    done = 0
    for size in (4, 5, 6):
        owners = [gblk_at(move) for move in moves[done : done + size]]
        done += size
        fill_slots(owners)

        @pl.when(p < ng)
        def _(owners=owners):
            for o in owners:
                owner_copy(o).start()

    fill_slots([p])
    own = pltpu.make_async_copy(send.at[p], out_ref.at[:, my_slots], own_sem)
    own.start()

    @pl.when(core == 0)
    def _():
        energies_copy(pairs - 1, 0).wait_send()
        many_copy(pairs - 1, gs_sem, fr_sem).wait_send()
        many_copy(pairs - 1, fs_sem, fr_sem).wait_send()

    @pl.when(core == 1)
    def _():
        energies_copy(pairs, 0).wait_send()
        many_copy(pairs, gs_sem, fr_sem).wait_send()
        many_copy(pairs, fs_sem, fr_sem).wait_send()

    energies_copy(pairs, 1).wait_send()

    @pl.when(p == 0)
    def _():
        for i in range(ng // 2):
            window_copy(i, partner).wait_send()

    @pl.when((core == 0) & (p > 0))
    def _():
        window_copy(0, partner).wait_send()

    own.wait()
    others = (ng - 1) * CAP * BLK
    all_copies = pltpu.make_async_remote_copy(
        src_ref=send.at[pl.ds(0, ng - 1)],
        dst_ref=out_ref.at[:, pl.ds(0, others)],
        send_sem=cs_sem,
        recv_sem=cr_sem,
        device_id={"gblk": partner},
    )
    all_copies.wait_send()
    all_copies.wait_recv()


def per_device(nb, ng, psi_val, psi_con, val_energy, con_energy, sphere_basis, block_owner, block_fill):
    r, cols = sphere_basis.shape
    blocks = cols // BLK
    factor = 1.0 / math.sqrt(psi_val.shape[0] * nb * psi_con.shape[0] * nb)
    hbm = pl.BlockSpec(memory_space=pltpu.HBM)
    args = (psi_val, psi_con, val_energy, con_energy, block_owner, block_fill, sphere_basis)
    args = [pltpu.with_memory_space_constraint(a, pltpu.HBM) for a in args]
    slot_cols = ng * CAP * BLK
    dma = pltpu.SemaphoreType.DMA
    got = pl.pallas_call(
        functools.partial(kernel, nb, ng, factor),
        out_shape=jax.ShapeDtypeStruct((WIN, slot_cols), bf16),
        in_specs=[hbm] * len(args),
        out_specs=pl.BlockSpec(memory_space=pl.ANY),
        scratch_shapes=[
            pltpu.SMEM(val_energy.shape, f32),
            pltpu.SMEM(con_energy.shape, f32),
            pltpu.SMEM(block_owner.shape, jnp.int32),
            pltpu.SMEM(block_fill.shape, jnp.int32),
            pltpu.VMEM((VAL, r), bf16),
            pltpu.VMEM((CON, r), bf16),
            pltpu.VMEM((blocks, r, BLK), bf16),
            pltpu.VMEM((r, BLK), bf16),
            pltpu.VMEM((nb * GROUP, r * (VAL + CON) // GROUP), bf16),
            pltpu.VMEM((2, nb // 2, 2, BLK), f32),
            pltpu.VMEM((2, BLK), f32),
            pltpu.VMEM((BLK, r), f32),
            pltpu.VMEM((WIN, r), bf16),
            pltpu.VMEM((nb * VAL, r), bf16),
            pltpu.VMEM((nb * CON, r), f32),
            pltpu.VMEM((WIN * nb * CON, r), bf16),
            pltpu.VMEM((WIN * nb * CON, nb * VAL), bf16),
            pltpu.VMEM((WIN, r), f32),
            pltpu.VMEM((ng, WIN, CAP * BLK), bf16),
            pltpu.SMEM((ng * CAP,), jnp.int32),
            dma((7,)),
            dma(()),
            dma(()),
            dma((nb // 2,)),
            dma(()),
            dma(()),
            dma((2,)),
            dma((2,)),
            dma((ng // 2,)),
            dma(()),
            dma(()),
            dma(()),
            dma(()),
        ],
        name="polarizability",
        compiler_params=pltpu.CompilerParams(
            collective_id=0, has_side_effects=True, vmem_limit_bytes=48 * 1024 * 1024
        ),
    )(*args)
    return got.astype(f32).T


def solution(mesh):
    nb, ng = mesh.shape["band"], mesh.shape["gblk"]
    return jax.shard_map(
        functools.partial(per_device, nb, ng),
        mesh=mesh,
        in_specs=(
            P("band", None),
            P("band", None),
            P("band"),
            P("band"),
            P(None, "gblk"),
            P(),
            P(),
        ),
        out_specs=P("gblk", "band"),
        check_vma=False,
    )
```

```python
import functools
import math

import jax
import jax.numpy as jnp
from jax import lax
from jax.experimental import pallas as pl
from jax.experimental.pallas import tpu as pltpu
from jax.sharding import PartitionSpec as P

BLK = 128
CAP = 3
GROUP = 16
VAL = 8
CON = 4
WIN = 16

f32 = jnp.float32
bf16 = jnp.bfloat16


def kernel(
    nb,
    ng,
    factor,
    val_hbm,
    con_hbm,
    ve_hbm,
    ce_hbm,
    owner_hbm,
    fill_hbm,
    table_hbm,
    out_ref,
    ve_ref,
    ce_ref,
    owner_ref,
    fill_ref,
    val_v,
    con_v,
    table_v,
    win_v,
    packed,
    energy,
    mine_e,
    turned,
    bw,
    val_m,
    con_f,
    x_s,
    s_s,
    m_s,
    send,
    slot_s,
    ld_sem,
    tb_sem,
    gs_sem,
    gr_sem,
    fs_sem,
    fr_sem,
    es_sem,
    er_sem,
    ws_sem,
    wr_sem,
    cs_sem,
    cr_sem,
    own_sem,
):
    b = lax.axis_index("band")
    p = lax.axis_index("gblk")
    core = lax.rem(p, 2)
    partner = p + 1 - 2 * core
    r = val_v.shape[1]
    vals, cons = nb * VAL, nb * CON
    val_cols, con_cols = r * VAL // GROUP, r * CON // GROUP
    blocks = table_v.shape[0]
    pairs = nb // 2
    z, y = b // 2, lax.rem(b, 2)
    x, y_hi = p // 4, lax.rem(p // 2, 2)
    turns = ng // 4

    steps = sorted(range(pairs), key=lambda i: -min(i, pairs - i))
    moves = [(dx, dy, dc) for dx in range(turns) for dy in range(2) for dc in range(2)][1:]
    moves.sort(key=lambda m: -(min(m[0], turns - m[0]) + 2 * m[1] + 0.1 * m[2]))

    def band_at(i, flip):
        return 2 * lax.rem(z + i, pairs) + lax.rem(y + flip, 2)

    def gblk_at(move):
        dx, dy, dc = move
        return 4 * lax.rem(x + dx, turns) + 2 * lax.rem(y_hi + dy, 2) + lax.rem(core + dc, 2)

    barrier = pltpu.get_barrier_semaphore()
    for i in steps:
        for flip in (1, 0):
            if i or flip:
                pl.semaphore_signal(barrier, 1, device_id={"band": band_at(i, flip)})
    for move in moves:
        pl.semaphore_signal(barrier, 1, device_id={"gblk": gblk_at(move)})

    ld_val = pltpu.make_async_copy(val_hbm, val_v, ld_sem.at[0])
    ld_con = pltpu.make_async_copy(con_hbm, con_v, ld_sem.at[1])
    ld_ve = pltpu.make_async_copy(ve_hbm, ve_ref, ld_sem.at[2])
    ld_ce = pltpu.make_async_copy(ce_hbm, ce_ref, ld_sem.at[3])
    ld_owner = pltpu.make_async_copy(owner_hbm, owner_ref, ld_sem.at[4])
    ld_fill = pltpu.make_async_copy(fill_hbm, fill_ref, ld_sem.at[5])
    wcol = pl.multiple_of((b // (BLK // WIN)) * BLK, BLK)

    def win_copy():
        return pltpu.make_async_copy(table_hbm.at[:, pl.ds(wcol, BLK)], win_v, ld_sem.at[6])

    for load in (ld_ve, ld_ce, ld_val, ld_con):
        load.start()

    @pl.when(p == 0)
    def _():
        win_copy().start()

    ld_owner.start()
    ld_fill.start()
    for j in range(blocks):
        pltpu.make_async_copy(
            table_hbm.at[:, j * BLK : (j + 1) * BLK], table_v.at[j], tb_sem
        ).start()

    lane = lax.broadcasted_iota(jnp.int32, (1, BLK), 1)
    mine_v = jnp.zeros((1, BLK), f32)
    mine_c = jnp.zeros((1, BLK), f32)
    ld_ve.wait()
    ld_ce.wait()
    for j in range(VAL):
        mine_v = jnp.where(lane % VAL == j, ve_ref[j], mine_v)
    for j in range(CON):
        mine_c = jnp.where(lane % CON == j, ce_ref[j], mine_c)
    mine_e[...] = jnp.concatenate([mine_v, mine_c], axis=0)

    @pl.when(core == 0)
    def _():
        energy[y, z] = mine_e[...]

    ld_val.wait()
    ld_con.wait()
    val_f = val_v[...].astype(f32)
    con_g = con_v[...].astype(f32)
    val_f = jnp.concatenate([val_f[:, i : i + val_cols] for i in range(0, r, val_cols)], axis=0)
    con_g = jnp.concatenate([con_g[:, i : i + con_cols] for i in range(0, r, con_cols)], axis=0)

    def rows_of(group):
        return pl.ds(pl.multiple_of(group * GROUP, GROUP), GROUP)

    packed[rows_of(b), :] = jnp.concatenate([val_f, con_g], axis=1).astype(bf16)

    @pl.when(p == 0)
    def _():
        win_copy().wait()
        turned[...] = win_v[...].astype(f32).T
        first = pl.multiple_of(lax.rem(b, BLK // WIN) * WIN, WIN)
        bw[...] = turned[pl.ds(first, WIN), :].astype(bf16)

    pl.semaphore_wait(barrier, nb + ng - 2)

    def gather_copy(i, group):
        return pltpu.make_async_remote_copy(
            src_ref=packed.at[rows_of(group)],
            dst_ref=packed.at[rows_of(group)],
            send_sem=gs_sem,
            recv_sem=gr_sem.at[i],
            device_id={"band": band_at(i, core)},
        )

    def forward_copy(group):
        return pltpu.make_async_remote_copy(
            src_ref=packed.at[rows_of(group)],
            dst_ref=packed.at[rows_of(group)],
            send_sem=fs_sem,
            recv_sem=fr_sem,
            device_id={"gblk": partner},
        )

    def many_copy(count, send_sem, recv_sem):
        rows = packed.at[pl.ds(0, count * GROUP)]
        return pltpu.make_async_remote_copy(
            src_ref=rows,
            dst_ref=rows,
            send_sem=send_sem,
            recv_sem=recv_sem,
            device_id={"gblk": partner},
        )

    def energy_copy(i):
        return pltpu.make_async_remote_copy(
            src_ref=mine_e,
            dst_ref=energy.at[y, z],
            send_sem=es_sem.at[0],
            recv_sem=er_sem.at[0],
            device_id={"band": band_at(i, core)},
        )

    def energies_copy(count, k):
        rows = energy.at[lax.rem(y + core, 2), pl.ds(0, count)]
        return pltpu.make_async_remote_copy(
            src_ref=rows,
            dst_ref=rows,
            send_sem=es_sem.at[k],
            recv_sem=er_sem.at[k],
            device_id={"gblk": partner},
        )

    def window_copy(i, target):
        return pltpu.make_async_remote_copy(
            src_ref=bw,
            dst_ref=bw,
            send_sem=ws_sem.at[i],
            recv_sem=wr_sem,
            device_id={"gblk": target},
        )

    @pl.when(p == 0)
    def _():
        for i in range(ng // 2 - 1, 0, -1):
            window_copy(i, 2 * i).start()

    early = 3
    for i in steps[:early]:
        gather_copy(i, b).start()
    for i in steps[:-1]:
        energy_copy(i).start()
    for i in steps[early:-1]:
        gather_copy(i, b).start()

    @pl.when(core == 1)
    def _():
        energy_copy(0).start()
        gather_copy(0, b).start()

    @pl.when(p == 0)
    def _():
        window_copy(0, partner).start()

    def slots_of(o, carry):
        count = jnp.int32(0)
        first = jnp.int32(blocks)
        second = jnp.int32(blocks)
        third = jnp.int32(blocks)
        for j in range(blocks):
            hit = owner_ref[p * blocks + j] == o
            first = jnp.where(hit & (count == 0), j, first)
            second = jnp.where(hit & (count == 1), j, second)
            third = jnp.where(hit & (count == 2), j, third)
            count = count + jnp.where(hit, 1, 0)
        slot_s[o * CAP] = first
        slot_s[o * CAP + 1] = second
        slot_s[o * CAP + 2] = third
        return carry

    ld_owner.wait()
    ld_fill.wait()
    lax.fori_loop(0, ng, slots_of, 0)

    def pass_on(i):
        group = band_at(pairs - i, core)
        gather_copy(i, group).wait_recv()
        forward_copy(group).start()

    for i in steps[:4]:
        pass_on(i)

    @pl.when(core == 0)
    def _():
        energies_copy(pairs - 1, 0).wait_recv()

    @pl.when(core == 1)
    def _():
        energies_copy(pairs, 0).wait_recv()

    energies_copy(pairs, 1).start()
    for i in steps[4:-1]:
        pass_on(i)

    @pl.when(core == 1)
    def _():
        pass_on(0)

    @pl.when(p > 0)
    def _():
        window_copy(0, partner).wait_recv()

    @pl.when((core == 0) & (p > 0))
    def _():
        window_copy(0, partner).start()

    energies_copy(pairs, 1).wait_recv()

    on_lanes = jnp.zeros((1, vals), f32)
    con_lanes = jnp.zeros((1, vals), f32)
    for g in range(nb):
        both = energy[g % 2, g // 2]
        on_lanes = jnp.where(lane // VAL == g, both[0:1], on_lanes)
        con_lanes = jnp.where(lane // CON == g, both[1:2], con_lanes)
    clane = lax.broadcasted_iota(jnp.int32, (cons, vals), 1)
    crow = lax.broadcasted_iota(jnp.int32, (cons, vals), 0)
    on_rows = jnp.sum(jnp.where(clane == crow, con_lanes, 0.0), axis=1, keepdims=True)
    weight = factor / (on_lanes - on_rows)
    wrow = lax.broadcasted_iota(jnp.int32, (WIN, 1), 0) + lax.rem(b, BLK // WIN) * WIN
    win_live = (wrow < fill_ref[b // (BLK // WIN)]).astype(f32)
    window = bw[...].astype(f32) * win_live

    @pl.when(core == 0)
    def _():
        many_copy(pairs, fs_sem, fr_sem).wait_recv()

    @pl.when(core == 1)
    def _():
        many_copy(pairs - 1, fs_sem, fr_sem).wait_recv()

    for g in range(0, nb, 2):
        one = packed[g * GROUP : (g + 1) * GROUP, :].astype(f32)
        two = packed[(g + 1) * GROUP : (g + 2) * GROUP, :].astype(f32)
        for i in range(r // val_cols):
            both = jnp.concatenate(
                [t[i * VAL : (i + 1) * VAL, 0:val_cols] for t in (one, two)], axis=0
            )
            val_m[g * VAL : (g + 2) * VAL, i * val_cols : (i + 1) * val_cols] = both.astype(bf16)
        for i in range(r // con_cols):
            both = jnp.concatenate(
                [t[i * CON : (i + 1) * CON, val_cols:] for t in (one, two)], axis=0
            )
            con_f[g * CON : (g + 2) * CON, i * con_cols : (i + 1) * con_cols] = both

    for h in range(WIN):
        x_s[h * cons : (h + 1) * cons, :] = (con_f[...] * window[h : h + 1, :]).astype(bf16)
    group_h = 4
    rows_h = group_h * cons
    weight_t = jnp.concatenate([weight] * group_h, axis=0)
    for q in range(WIN // group_h):
        chunk = slice(q * rows_h, (q + 1) * rows_h)
        raw = lax.dot_general(
            x_s[chunk, :], val_m[...], (((1,), (1,)), ((), ())), preferred_element_type=f32
        )
        s_s[chunk, :] = (raw * weight_t).astype(bf16)
    for q in range(WIN // group_h):
        chunk = slice(q * rows_h, (q + 1) * rows_h)
        full = jnp.dot(s_s[chunk, :], val_m[...], preferred_element_type=f32)
        for i in range(group_h):
            part = full[i * cons : (i + 1) * cons, :] * con_f[...]
            h = q * group_h + i
            m_s[h : h + 1, :] = jnp.sum(part, axis=0, keepdims=True)

    m_hi = m_s[...].astype(bf16)
    m_lo = (m_s[...] - m_hi.astype(f32)).astype(bf16)
    m_two = jnp.concatenate([m_hi, m_lo], axis=0)

    my_slots = pl.ds(pl.multiple_of(p * CAP * BLK, CAP * BLK), CAP * BLK)

    def owner_copy(o):
        return pltpu.make_async_remote_copy(
            src_ref=send.at[o],
            dst_ref=out_ref.at[:, my_slots],
            send_sem=cs_sem,
            recv_sem=cr_sem,
            device_id={"gblk": o},
        )

    lanes = lax.broadcasted_iota(jnp.int32, (1, CAP * BLK), 1)

    def fill_slots(owners):
        table = []
        limits = []
        for o in owners:
            limit = jnp.zeros((1, CAP * BLK), jnp.int32)
            for s in range(CAP):
                block = slot_s[o * CAP + s]
                j = jnp.minimum(block, blocks - 1)
                live = jnp.where(block < blocks, fill_ref[p * blocks + j], 0)
                limit = jnp.where(lanes // BLK == s, live, limit)
                table.append(table_v[j])
            limits.append(limit)
        wide = jnp.dot(m_two, jnp.concatenate(table, axis=1), preferred_element_type=f32)
        wide = wide[0:WIN] + wide[WIN:]
        for i, o in enumerate(owners):
            rows = wide[:, i * CAP * BLK : (i + 1) * CAP * BLK]
            send[o] = jnp.where(lanes % BLK < limits[i], rows, 0.0).astype(bf16)

    pltpu.make_async_copy(table_v, table_v, tb_sem).wait()

    done = 0
    for size in (4, 5, 6):
        owners = [gblk_at(move) for move in moves[done : done + size]]
        done += size
        fill_slots(owners)

        @pl.when(p < ng)
        def _(owners=owners):
            for o in owners:
                owner_copy(o).start()

    fill_slots([p])
    own = pltpu.make_async_copy(send.at[p], out_ref.at[:, my_slots], own_sem)
    own.start()

    @pl.when(core == 0)
    def _():
        energies_copy(pairs - 1, 0).wait_send()
        many_copy(pairs - 1, gs_sem, fr_sem).wait_send()
        many_copy(pairs - 1, fs_sem, fr_sem).wait_send()

    @pl.when(core == 1)
    def _():
        energies_copy(pairs, 0).wait_send()
        many_copy(pairs, gs_sem, fr_sem).wait_send()
        many_copy(pairs, fs_sem, fr_sem).wait_send()

    energies_copy(pairs, 1).wait_send()

    @pl.when(p == 0)
    def _():
        for i in range(ng // 2):
            window_copy(i, partner).wait_send()

    @pl.when((core == 0) & (p > 0))
    def _():
        window_copy(0, partner).wait_send()

    own.wait()
    others = (ng - 1) * CAP * BLK
    all_copies = pltpu.make_async_remote_copy(
        src_ref=send.at[pl.ds(0, ng - 1)],
        dst_ref=out_ref.at[:, pl.ds(0, others)],
        send_sem=cs_sem,
        recv_sem=cr_sem,
        device_id={"gblk": partner},
    )
    all_copies.wait_send()
    all_copies.wait_recv()


def per_device(nb, ng, psi_val, psi_con, val_energy, con_energy, sphere_basis, block_owner, block_fill):
    r, cols = sphere_basis.shape
    blocks = cols // BLK
    factor = 1.0 / math.sqrt(psi_val.shape[0] * nb * psi_con.shape[0] * nb)
    hbm = pl.BlockSpec(memory_space=pltpu.HBM)
    args = (psi_val, psi_con, val_energy, con_energy, block_owner, block_fill, sphere_basis)
    args = [pltpu.with_memory_space_constraint(a, pltpu.HBM) for a in args]
    slot_cols = ng * CAP * BLK
    dma = pltpu.SemaphoreType.DMA
    got = pl.pallas_call(
        functools.partial(kernel, nb, ng, factor),
        out_shape=jax.ShapeDtypeStruct((WIN, slot_cols), bf16),
        in_specs=[hbm] * len(args),
        out_specs=pl.BlockSpec(memory_space=pl.ANY),
        scratch_shapes=[
            pltpu.SMEM(val_energy.shape, f32),
            pltpu.SMEM(con_energy.shape, f32),
            pltpu.SMEM(block_owner.shape, jnp.int32),
            pltpu.SMEM(block_fill.shape, jnp.int32),
            pltpu.VMEM((VAL, r), bf16),
            pltpu.VMEM((CON, r), bf16),
            pltpu.VMEM((blocks, r, BLK), bf16),
            pltpu.VMEM((r, BLK), bf16),
            pltpu.VMEM((nb * GROUP, r * (VAL + CON) // GROUP), bf16),
            pltpu.VMEM((2, nb // 2, 2, BLK), f32),
            pltpu.VMEM((2, BLK), f32),
            pltpu.VMEM((BLK, r), f32),
            pltpu.VMEM((WIN, r), bf16),
            pltpu.VMEM((nb * VAL, r), bf16),
            pltpu.VMEM((nb * CON, r), f32),
            pltpu.VMEM((WIN * nb * CON, r), bf16),
            pltpu.VMEM((WIN * nb * CON, nb * VAL), bf16),
            pltpu.VMEM((WIN, r), f32),
            pltpu.VMEM((ng, WIN, CAP * BLK), bf16),
            pltpu.SMEM((ng * CAP,), jnp.int32),
            dma((7,)),
            dma(()),
            dma(()),
            dma((nb // 2,)),
            dma(()),
            dma(()),
            dma((2,)),
            dma((2,)),
            dma((ng // 2,)),
            dma(()),
            dma(()),
            dma(()),
            dma(()),
        ],
        name="polarizability",
        compiler_params=pltpu.CompilerParams(
            collective_id=0, has_side_effects=True, vmem_limit_bytes=48 * 1024 * 1024
        ),
    )(*args)
    return got.astype(f32).T


def solution(mesh):
    nb, ng = mesh.shape["band"], mesh.shape["gblk"]
    return jax.shard_map(
        functools.partial(per_device, nb, ng),
        mesh=mesh,
        in_specs=(
            P("band", None),
            P("band", None),
            P("band"),
            P("band"),
            P(None, "gblk"),
            P(),
            P(),
        ),
        out_specs=P("gblk", "band"),
        check_vma=False,
    )
```
